256 devices in a mesh: wave: 64 (over y, z, core), lev: 4 (over x).
Axes of the slice: x: 4, y: 4, z: 8, core: 2. Of those that a mesh axis runs over, the one named last changes fastest.
Arguments:
- spectral_even: bfloat16 [640, 641, 512], P('wave', None, 'lev'), may hold values from -0.125 to 0.125
- spectral_odd: bfloat16 [640, 640, 512], P('wave', None, 'lev'), may hold values from -0.125 to 0.125
- table_even: bfloat16 [640, 641, 128], P('wave'), may hold values from -0.15625 to 0.15625
- table_odd: bfloat16 [640, 640, 128], P('wave'), may hold values from -0.15625 to 0.15625
- slot_pair: int32 [640], replicated, may hold values from 0 to 639, each once
- slot_row: int32 [256], replicated, may hold values from 0 to 255, each once
- row_length: int32 [128], replicated, may hold values from 20 to 5136, as said below
Outputs:
- grid: bfloat16 [256, 256, 5632], P(('wave', 'lev'))
The draws below stay inside these ranges and needn't reach their ends.
Inputs may be any that keep to these rules, and one draw needn't show every extreme that they name: `row_length`: each value is 4 j + 16 for a latitude index j from 1 to 1280, distinct over pairs; j = 1 and j = 1280 always occur.
All inputs are finite; a program needn't handle non-finite values.
Results may differ from the reference program's by a relative error of at most 0.0055.
Values may be sent and summed in bfloat16 or wider, within the bound.
A program may use at most 192 MiB of HBM per device.

```python
import math
import jax
import jax.numpy as jnp
from jax import lax

TRUNC = 1280
SLOTS = 640
EVEN_K = 641
ODD_K = 640
LEVELS = 256
ROWS = 256
PAIRS = 128
LPAD = 5632


def draw_row_length(key, part):
    key = jax.random.fold_in(key, 7)
    first_key, second_key = jax.random.split(key)
    inner = jax.random.permutation(first_key, TRUNC - 2)[:PAIRS - 2].astype(jnp.int32) + 2
    latitude = jnp.concatenate([jnp.array([TRUNC, 1], jnp.int32), inner])
    shuffled = latitude[jax.random.permutation(second_key, PAIRS)]
    return (4 * shuffled + 16).astype(jnp.int32)


def block_levels(stream_key, shape, shards, least, top_value):
    def one(dim, parts):
        draws = jax.random.uniform(jax.random.fold_in(jax.random.fold_in(stream_key, 6), dim), (parts,), jnp.float32, least / len(shards), top_value / len(shards))
        return jnp.repeat(jnp.exp(draws), shape[dim] // parts).reshape((-1,) + (1,) * (len(shape) - dim - 1))

    factor_of = one(*shards[0])
    for cut in shards[1:]:
        factor_of = factor_of * one(*cut)
    return factor_of


def scatter_about(key, extent, width, limit, pieces=(), kind=jnp.bfloat16):
    level = block_levels(key, extent, pieces, -0.22, 0.18) if pieces else 1.0
    drawn = jax.random.normal(key, extent, jnp.float32) * width * level
    return jnp.minimum(jnp.maximum(drawn, -limit), limit).astype(kind)


def setup_inputs(seed: int = 0) -> dict:
    splits = jax.random.split(jax.random.key(seed), 8)
    return {
        "spectral_even": scatter_about(splits[0], (SLOTS, EVEN_K, 2 * LEVELS), (2 * TRUNC) ** -0.5, 0.125, ((0, 64), (2, 4))),
        "spectral_odd": scatter_about(splits[1], (SLOTS, ODD_K, 2 * LEVELS), (2 * TRUNC) ** -0.5, 0.125, ((0, 64), (2, 4))),
        "table_even": scatter_about(splits[2], (SLOTS, EVEN_K, PAIRS), (TRUNC + 1) ** -0.5, 0.15625, ((0, 64),)),
        "table_odd": scatter_about(splits[3], (SLOTS, ODD_K, PAIRS), (TRUNC + 1) ** -0.5, 0.15625, ((0, 64),)),
        "slot_pair": jax.random.permutation(splits[4], SLOTS).astype(jnp.int32),
        "slot_row": jax.random.permutation(splits[5], ROWS).astype(jnp.int32),
        "row_length": draw_row_length(jax.random.fold_in(splits[7], 71), 0),
    }


def split_terms(table, coeffs, count):
    position = jnp.arange(table.shape[0], dtype=jnp.int32)
    inside = (position < count)[:, None]
    coeffs = coeffs.astype(jnp.float32)
    zeroes = jnp.zeros_like(coeffs)
    stacked = jnp.stack([jnp.where(inside, coeffs, zeroes), jnp.where(inside, zeroes, coeffs)], axis=1)
    return jnp.einsum("kp,kwc->wpc", table.astype(jnp.float32), stacked)


def reference(spectral_even, spectral_odd, table_even, table_odd, slot_pair, slot_row, row_length):
    pairs = row_length.shape[0]

    def one_slot(packed):
        coeff_even, coeff_odd, tab_even, tab_odd, first = packed
        sym_part = split_terms(tab_even, coeff_even, (TRUNC + 1 - first) // 2)
        anti_part = split_terms(tab_odd, coeff_odd, (TRUNC - first) // 2)
        return jnp.concatenate([sym_part + anti_part, sym_part - anti_part], axis=1).astype(jnp.bfloat16)

    fourier = lax.map(one_slot, (spectral_even, spectral_odd, table_even, table_odd, slot_pair))
    wavenums = jnp.stack([slot_pair, TRUNC - 1 - slot_pair], axis=1).reshape(-1).astype(jnp.int32)
    points = jnp.arange(LPAD, dtype=jnp.int32)

    def one_row(row):
        length = row_length[row % pairs]
        columns = fourier[:, :, row, :].reshape(TRUNC, -1, 2).astype(jnp.float32)
        product = (wavenums[None, :] * points[:, None]) % length
        phase = product.astype(jnp.float32) * (2.0 * math.pi) / length.astype(jnp.float32)
        active = 2 * wavenums < length
        factor = jnp.where(active, jnp.where(wavenums == 0, 1.0, 2.0), 0.0).astype(jnp.float32)
        basis = jnp.stack([factor[None, :] * jnp.cos(phase), -factor[None, :] * jnp.sin(phase)], axis=-1).astype(jnp.bfloat16)
        values = jnp.einsum("kmr,mvr->vk", basis.astype(jnp.float32), columns)
        return jnp.where(points[None, :] < length, values, 0.0).astype(jnp.bfloat16)

    return lax.map(one_row, slot_row)
```

```python
import math

import jax
import jax.numpy as jnp
from jax import lax
from jax.experimental import pallas as pl
from jax.experimental.pallas import tpu as pltpu
from jax.sharding import PartitionSpec as P

TRUNC = 1280
SLOTS = 640
LPAD = 5632
ROWS = 256
PAIRS = 128
WAVE = 64
LEV = 4
SLOTS_DEV = 10
MESSAGE = 2 * SLOTS_DEV
STEP_SLOTS = 2
STEPS = SLOTS_DEV // STEP_SLOTS
QUARTER_PAD = 1536
LANES = 128
BLOCK = 256
BLOCKS = QUARTER_PAD // BLOCK
CHUNK = 8

MESH = pl.DeviceIdType.MESH
VMEM = pltpu.VMEM
SMEM = pltpu.SMEM
F32 = jnp.float32
BF16 = jnp.bfloat16
TN = (((0,), (0,)), ((), ()))
NT = (((1,), (1,)), ((), ()))


def lane_iota(rows):
    return lax.broadcasted_iota(jnp.int32, (rows, LANES), 1)


def unit_circle(product, length, inverse):
    rest = product - jnp.floor(product * inverse) * length
    quarters = rest * (4.0 * inverse)
    nearest = jnp.floor(quarters + 0.5)
    angle = (quarters - nearest) * (0.5 * math.pi)
    z = angle * angle
    sine = angle * (1.0 + z * (-1.0 / 6 + z * (1.0 / 120 + z * (-1.0 / 5040 + z * (1.0 / 362880)))))
    cosine = 1.0 + z * (-0.5 + z * (1.0 / 24 + z * (-1.0 / 720 + z * (1.0 / 40320))))
    quadrant = nearest.astype(jnp.int32)
    odd = (quadrant & 1) == 1
    cos_out = jnp.where(odd, sine, cosine)
    sin_out = jnp.where(odd, cosine, sine)
    cos_out = jnp.where(((quadrant + 1) & 2) == 2, -cos_out, cos_out)
    sin_out = jnp.where((quadrant & 2) == 2, -sin_out, sin_out)
    return cos_out, sin_out


def masked_halves(coeffs, count, flip):
    rows = coeffs.shape[0]
    position = lax.broadcasted_iota(jnp.int32, (rows, LANES), 0)
    first = jnp.where(position < count, 1.0, 0.0)
    chosen = (flip + (1.0 - 2.0 * flip) * first).astype(BF16)
    even = coeffs * chosen
    return jnp.concatenate([even, coeffs - even], axis=1)


def exchange_kernel(
    pair_s,
    row_s,
    length_s,
    pair_v,
    row_v,
    spec_even,
    spec_odd,
    tab_even,
    tab_odd,
    recv,
    basis_out,
    permute,
    spread,
    send,
    waves,
    basis,
    send_sem,
    recv_sem,
    self_sem,
    basis_sem,
    line_sem,
):
    step = pl.program_id(0)
    w = lax.axis_index("wave")
    l = lax.axis_index("lev")
    me = w * LEV + l
    my_slot = l * WAVE + w
    barrier = pltpu.get_barrier_semaphore()

    @pl.when(step == 0)
    def _():
        def greet(i, carry):
            pl.semaphore_signal(
                barrier, inc=1, device_id=(lax.rem(w + i, WAVE), l), device_id_type=MESH
            )
            return carry

        lax.fori_loop(1, WAVE, greet, 0)
        for i in range(1, LEV):
            pl.semaphore_signal(
                barrier, inc=1, device_id=(w, lax.rem(l + i, LEV)), device_id_type=MESH
            )
        source = lax.broadcasted_iota(jnp.int32, (ROWS, ROWS), 0)
        hot = jnp.where(source == row_v[...], 1.0, 0.0)
        permute[...] = hot.T.astype(BF16)

    @pl.when(step == STEPS - 2)
    def _():
        pl.semaphore_wait(barrier, WAVE - 1 + LEV - 1)
        for i in range(1, LEV):
            pl.semaphore_signal(
                line_sem, inc=1, device_id=(w, lax.rem(l + i, LEV)), device_id_type=MESH
            )

    for j in range(STEP_SLOTS):
        slot = step * STEP_SLOTS + j
        first = pair_s[w * SLOTS_DEV + slot]
        flip = (first & 1).astype(F32)
        even_terms = masked_halves(spec_even[j], (TRUNC + 1 - first) >> 1, flip)
        odd_terms = masked_halves(spec_odd[j], (TRUNC - first) >> 1, flip)
        sym = lax.dot_general(tab_even[j], even_terms, TN, preferred_element_type=F32)
        anti = lax.dot_general(tab_odd[j], odd_terms, TN, preferred_element_type=F32)
        rows = jnp.concatenate([sym + anti, sym - anti], axis=0).astype(BF16)
        ordered = jnp.dot(permute[...], rows, preferred_element_type=F32)
        spread[pl.ds(slot, ROWS, stride=MESSAGE), :] = ordered[:, :LANES]
        spread[pl.ds(slot + SLOTS_DEV, ROWS, stride=MESSAGE), :] = ordered[:, LANES:]

    @pl.when(step == STEPS - 1)
    def _():
        pl.semaphore_wait(line_sem, LEV - 1)

        def send_chunk(i, carry):
            chunk = lax.rem(me // CHUNK + i, ROWS // CHUNK)
            start = pl.multiple_of(chunk * CHUNK * MESSAGE, CHUNK * MESSAGE)
            block = spread[pl.ds(start, CHUNK * MESSAGE), :].astype(BF16)
            send[pl.ds(chunk * CHUNK, CHUNK)] = block.reshape(CHUNK, MESSAGE // 2, 2, LANES)
            for j in range(CHUNK):
                target = chunk * CHUNK + lax.rem(me + j, CHUNK)

                @pl.when(target != me)
                def _():
                    pltpu.make_async_remote_copy(
                        src_ref=send.at[target],
                        dst_ref=recv.at[my_slot],
                        send_sem=send_sem,
                        recv_sem=recv_sem,
                        device_id=(target // LEV, lax.rem(target, LEV)),
                        device_id_type=MESH,
                    ).start()

            return carry

        lax.fori_loop(0, ROWS // CHUNK, send_chunk, 0)
        own = pltpu.make_async_copy(send.at[me], recv.at[my_slot], self_sem)
        own.start()

        length = length_s[row_s[me] & (PAIRS - 1)].astype(F32)
        inverse = 1.0 / jnp.full((16, LANES), length, F32)
        for i in range(SLOTS // LANES):
            pair = pair_v[:, i * LANES : (i + 1) * LANES]
            even = jnp.where((pair & 1) == 0, pair, TRUNC - 1 - pair).astype(F32)
            waves[i * LANES : (i + 1) * LANES, :] = jnp.broadcast_to(even, (LANES, LANES)).T

        lane = lane_iota(16).astype(F32)

        def basis_rows(i, carry):
            at = pl.multiple_of(i * 16, 16)
            even = waves[pl.ds(at, 16), :]
            for parity in range(2):
                number = even if parity == 0 else (TRUNC - 1.0) - even
                factor = jnp.where(
                    2.0 * number < length, jnp.where(number == 0.0, 1.0, 2.0), 0.0
                )
                cosine, sine = unit_circle(number * lane, length, inverse)
                turn_cos, turn_sin = unit_circle(number * float(LANES), length, inverse)
                real = factor * cosine
                imag = -factor * sine
                for k in range(QUARTER_PAD // LANES):
                    columns = slice(k * LANES, (k + 1) * LANES)
                    basis[parity, pl.ds(at, 16), columns] = real.astype(BF16)
                    low = pl.multiple_of(at + SLOTS, 16)
                    basis[parity, pl.ds(low, 16), columns] = imag.astype(BF16)
                    real, imag = (
                        real * turn_cos + imag * turn_sin,
                        imag * turn_cos - real * turn_sin,
                    )
            return carry

        lax.fori_loop(0, SLOTS // 16, basis_rows, 0)
        out = pltpu.make_async_copy(basis, basis_out, basis_sem)
        out.start()

        own.wait()
        others = pl.ds(0, ROWS - 1)
        pltpu.make_async_copy(send.at[others], recv.at[others], recv_sem).wait()
        pltpu.make_async_copy(send.at[others], recv.at[others], send_sem).wait()
        out.wait()


def fourier_kernel(row_s, length_s, pair_v, recv, basis, grid_out, left, total):
    step = pl.program_id(0)
    me = lax.axis_index("wave") * LEV + lax.axis_index("lev")
    quarter = length_s[row_s[me] & (PAIRS - 1)] >> 2

    @pl.when(step == 0)
    def _():
        total[...] = jnp.zeros_like(total)
        row = lax.broadcasted_iota(jnp.int32, (LANES, LANES), 0)
        column = lane_iota(LANES)
        wanted = jnp.where(row < 64, 2 * row, 2 * row - 127)
        pick = jnp.where(column == wanted, 1.0, 0.0).astype(BF16)
        pair = pair_v[...]
        for parity in range(2):
            number = jnp.where((pair & 1) == parity, pair, TRUNC - 1 - pair)
            second = ((number >> 1) & 1).astype(F32)
            sign = 1.0 - 2.0 * second if parity == 0 else 2.0 * second - 1.0
            for l in range(LEV):
                block = recv[l * WAVE : (l + 1) * WAVE, parity * 5 : parity * 5 + 5]
                block = block.reshape(SLOTS, LANES)
                parts = lax.dot_general(pick, block, NT, preferred_element_type=F32)
                real, imag = parts[:64], parts[64:]
                top = slice(l * 64, l * 64 + 64)
                low = slice(256 + l * 64, 256 + l * 64 + 64)
                left[parity, top, :SLOTS] = real.astype(BF16)
                left[parity, top, SLOTS:] = imag.astype(BF16)
                if parity == 0:
                    left[parity, low, :SLOTS] = (real * sign).astype(BF16)
                    left[parity, low, SLOTS:] = (imag * sign).astype(BF16)
                else:
                    left[parity, low, :SLOTS] = (imag * sign).astype(BF16)
                    left[parity, low, SLOTS:] = (real * -sign).astype(BF16)

    even = jnp.dot(left[0], basis[0], preferred_element_type=F32)
    odd = jnp.dot(left[1], basis[1], preferred_element_type=F32)
    point = step * BLOCK + lax.broadcasted_iota(jnp.int32, (256, BLOCK), 1)
    inside = point < quarter
    lane = lane_iota(256)
    for c in range(4):
        half = slice((c & 1) * 256, (c & 1) * 256 + 256)
        value = even[half] + odd[half] if c < 2 else even[half] - odd[half]
        value = jnp.where(inside, value, 0.0)
        offset = c * quarter + step * BLOCK
        shift = offset & (LANES - 1)
        start = pl.multiple_of(offset - shift, LANES)
        turned = [pltpu.roll(value[:, :LANES], shift, 1), pltpu.roll(value[:, LANES:], shift, 1)]
        before = lane < shift
        zero = jnp.zeros_like(turned[0])
        pieces = [
            jnp.where(before, zero, turned[0]),
            jnp.where(before, turned[0], turned[1]),
            jnp.where(before, turned[1], zero),
        ]
        for i, piece in enumerate(pieces):
            where = pl.ds(pl.multiple_of(start + i * LANES, LANES), LANES)
            total[:, where] += piece

    @pl.when(step == BLOCKS - 1)
    def _():
        grid_out[0] = total[:, :LPAD].astype(BF16)


def shards(spectral_even, spectral_odd, table_even, table_odd, slot_pair, slot_row, row_length):
    pair_row = slot_pair.reshape(1, SLOTS)
    order_row = slot_row.reshape(1, ROWS)
    in_smem = pl.BlockSpec(memory_space=SMEM)
    in_vmem = pl.BlockSpec(memory_space=VMEM)
    anywhere = pl.BlockSpec(memory_space=pl.ANY)

    def by_slot(array):
        return pl.BlockSpec((STEP_SLOTS,) + array.shape[1:], lambda i: (i, 0, 0))

    message = (MESSAGE // 2, 2, LANES)
    recv, basis = pl.pallas_call(
        exchange_kernel,
        grid=(STEPS,),
        out_shape=[
            jax.ShapeDtypeStruct((ROWS,) + message, BF16),
            jax.ShapeDtypeStruct((2, TRUNC, QUARTER_PAD), BF16),
        ],
        in_specs=[in_smem] * 3
        + [in_vmem] * 2
        + [by_slot(a) for a in (spectral_even, spectral_odd, table_even, table_odd)],
        out_specs=[anywhere, anywhere],
        scratch_shapes=[
            VMEM((ROWS, ROWS), BF16),
            VMEM((ROWS * MESSAGE, LANES), F32),
            VMEM((ROWS,) + message, BF16),
            VMEM((SLOTS, LANES), F32),
            VMEM((2, TRUNC, QUARTER_PAD), BF16),
            pltpu.SemaphoreType.DMA,
            pltpu.SemaphoreType.DMA,
            pltpu.SemaphoreType.DMA,
            pltpu.SemaphoreType.DMA,
            pltpu.SemaphoreType.REGULAR,
        ],
        name="legendre_exchange",
        compiler_params=pltpu.CompilerParams(
            collective_id=0, has_side_effects=True, vmem_limit_bytes=40 << 20
        ),
        cost_estimate=pl.CostEstimate(
            flops=2 * SLOTS_DEV * 1281 * 128 * 256, bytes_accessed=16 << 20, transcendentals=0
        ),
    )(
        slot_pair,
        slot_row,
        row_length,
        pair_row,
        order_row,
        spectral_even,
        spectral_odd,
        table_even,
        table_odd,
    )
    return pl.pallas_call(
        fourier_kernel,
        grid=(BLOCKS,),
        out_shape=jax.ShapeDtypeStruct((1, 256, LPAD), BF16),
        in_specs=[
            in_smem,
            in_smem,
            in_vmem,
            in_vmem,
            pl.BlockSpec((2, TRUNC, BLOCK), lambda i: (0, 0, i)),
        ],
        out_specs=pl.BlockSpec((1, 256, LPAD), lambda i: (0, 0, 0)),
        scratch_shapes=[
            VMEM((2, 512, TRUNC), BF16),
            VMEM((256, LPAD + 2 * LANES), F32),
        ],
        name="fourier",
        compiler_params=pltpu.CompilerParams(vmem_limit_bytes=40 << 20),
        cost_estimate=pl.CostEstimate(
            flops=4 * 512 * TRUNC * QUARTER_PAD, bytes_accessed=12 << 20, transcendentals=0
        ),
    )(slot_row, row_length, pair_row, recv, basis)


def solution(mesh):
    in_specs = (
        P("wave", None, "lev"),
        P("wave", None, "lev"),
        P("wave", None, None),
        P("wave", None, None),
        P(),
        P(),
        P(),
    )
    out_specs = P(("wave", "lev"), None, None)
    return jax.shard_map(shards, mesh=mesh, in_specs=in_specs, out_specs=out_specs, check_vma=False)
```

```python
import math

import jax
import jax.numpy as jnp
from jax import lax
from jax.experimental import pallas as pl
from jax.experimental.pallas import tpu as pltpu
from jax.sharding import PartitionSpec as P

TRUNC = 1280
SLOTS = 640
LPAD = 5632
ROWS = 256
PAIRS = 128
WAVE = 64
LEV = 4
SLOTS_DEV = 10
MESSAGE = 2 * SLOTS_DEV
LOADS = ((0, 2), (2, 4), (6, 4))
QUARTER_PAD = 1408
LANES = 128
COLUMN_BLOCKS = ((0, 512), (512, 512), (1024, 384))
ROW_CHUNK = 128
ARRIVALS = ((0, 32, 384, 0), (32, 24, 256, 768), (56, 8, 128, 1280))
TERMS = 1536
GROUP = 16
BARRIER_LOAD = 1

MESH = pl.DeviceIdType.MESH
VMEM = pltpu.VMEM
SMEM = pltpu.SMEM
F32 = jnp.float32
BF16 = jnp.bfloat16
TN = (((0,), (0,)), ((), ()))
NT = (((1,), (1,)), ((), ()))


def lane_iota(rows):
    return lax.broadcasted_iota(jnp.int32, (rows, LANES), 1)


def unit_circle(product, length, inverse):
    rest = product - jnp.floor(product * inverse) * length
    quarters = rest * (4.0 * inverse)
    nearest = jnp.floor(quarters + 0.5)
    angle = (quarters - nearest) * (0.5 * math.pi)
    z = angle * angle
    sine = angle * (1.0 + z * (-1.0 / 6 + z * (1.0 / 120 + z * (-1.0 / 5040 + z * (1.0 / 362880)))))
    cosine = 1.0 + z * (-0.5 + z * (1.0 / 24 + z * (-1.0 / 720 + z * (1.0 / 40320))))
    quadrant = nearest.astype(jnp.int32)
    odd = (quadrant & 1) == 1
    cos_out = jnp.where(odd, sine, cosine)
    sin_out = jnp.where(odd, cosine, sine)
    cos_out = jnp.where(((quadrant + 1) & 2) == 2, -cos_out, cos_out)
    sin_out = jnp.where((quadrant & 2) == 2, -sin_out, sin_out)
    return cos_out, sin_out


def masked_halves(coeffs, count, flip):
    rows = coeffs.shape[0]
    position = lax.broadcasted_iota(jnp.int32, (rows, LANES), 0)
    first = jnp.where(position < count, 1.0, 0.0)
    chosen = (flip + (1.0 - 2.0 * flip) * first).astype(BF16)
    even = coeffs * chosen
    return jnp.concatenate([even, coeffs - even], axis=1)


def exchange_kernel(
    pair_s,
    row_s,
    length_s,
    pair_v,
    row_v,
    spec_even_in,
    spec_odd_in,
    tab_even_in,
    tab_odd_in,
    quarters_out,
    spec_even,
    spec_odd,
    tab_even,
    tab_odd,
    permute,
    spread,
    send,
    recv,
    waves,
    basis,
    left,
    total,
    quarters,
    send_sem,
    recv_sem,
    self_sem,
    load_sem,
    out_sem,
    line_sem,
):
    w = lax.axis_index("wave")
    l = lax.axis_index("lev")
    me = w * LEV + l
    barrier = pltpu.get_barrier_semaphore()

    def in_plane(i):
        return (w - lax.rem(w, GROUP) + lax.rem(w + i, GROUP), l)

    def across(i):
        return (lax.rem(w + i // LEV * GROUP, WAVE), lax.rem(l + i, LEV))

    loads = []
    for number, (begin, count) in enumerate(LOADS):
        slots = pl.ds(begin, count)
        loads.append(
            [
                pltpu.make_async_copy(source.at[slots], held.at[slots], load_sem.at[i, number])
                for i, (source, held) in enumerate(
                    (
                        (spec_even_in, spec_even),
                        (tab_even_in, tab_even),
                        (spec_odd_in, spec_odd),
                        (tab_odd_in, tab_odd),
                    )
                )
            ]
        )
    for copy in loads[0]:
        copy.start()
    for i in range(1, GROUP):
        pl.semaphore_signal(barrier, inc=1, device_id=in_plane(i), device_id_type=MESH)
        pl.semaphore_signal(barrier, inc=1, device_id=across(i), device_id_type=MESH)
    for copies in loads[1:]:
        for copy in copies:
            copy.start()
    source = lax.broadcasted_iota(jnp.int32, (ROWS, ROWS), 0)
    hot = jnp.where(source == row_v[...].reshape(1, ROWS), 1.0, 0.0)
    permute[...] = hot.T.astype(BF16)

    def one_slot(slot):
        first = pair_s[w * SLOTS_DEV + slot]
        flip = (first & 1).astype(F32)
        even_terms = masked_halves(spec_even[slot], (TRUNC + 1 - first) >> 1, flip)
        odd_terms = masked_halves(spec_odd[slot], (TRUNC - first) >> 1, flip)
        sym = lax.dot_general(tab_even[slot], even_terms, TN, preferred_element_type=F32)
        anti = lax.dot_general(tab_odd[slot], odd_terms, TN, preferred_element_type=F32)
        rows = jnp.concatenate([sym + anti, sym - anti], axis=0).astype(BF16)
        ordered = jnp.dot(permute[...], rows, preferred_element_type=F32)
        spread[pl.ds(slot, ROWS, stride=MESSAGE), :] = ordered[:, :LANES]
        spread[pl.ds(slot + SLOTS_DEV, ROWS, stride=MESSAGE), :] = ordered[:, LANES:]

    for number, (begin, count) in enumerate(LOADS):
        for copy in loads[number]:
            copy.wait()

        def two_slots(i, carry, begin=begin):
            one_slot(begin + 2 * i)
            one_slot(begin + 2 * i + 1)
            return carry

        lax.fori_loop(0, count // 2, two_slots, 0)
        if number == BARRIER_LOAD:
            pl.semaphore_wait(barrier, 2 * (GROUP - 1))
            for i in range(1, GROUP):
                pl.semaphore_signal(line_sem, inc=1, device_id=across(i), device_id_type=MESH)

    pl.semaphore_wait(line_sem, GROUP - 1)

    def pack(back):
        target = lax.rem(w - back + WAVE, WAVE)
        start = pl.multiple_of(target * (LEV * MESSAGE), LEV * MESSAGE)
        block = spread[pl.ds(start, LEV * MESSAGE), :].astype(BF16)
        send[pl.ds(target * LEV, LEV)] = block.reshape(LEV, MESSAGE // 2, 2, LANES)
        return target

    def send_one(target, back, turn, part):
        lev = lax.rem(l - turn + LEV, LEV)
        pltpu.make_async_remote_copy(
            src_ref=send.at[target * LEV + lev],
            dst_ref=recv.at[l * WAVE + back],
            send_sem=send_sem,
            recv_sem=recv_sem.at[part],
            device_id=(target, lev),
            device_id_type=MESH,
        ).start()

    target = pack(0)
    for turn in range(1, LEV):
        send_one(target, 0, turn, 0)
    own = pltpu.make_async_copy(send.at[me], recv.at[l * WAVE], self_sem)
    own.start()
    for part, (begin, count, _, _) in enumerate(ARRIVALS):

        def send_four(back, carry, part=part):
            target = pack(back)
            for turn in range(LEV):
                send_one(target, back, turn, part)
            return carry

        lax.fori_loop(max(begin, 1), begin + count, send_four, 0)

    length = length_s[row_s[me] & (PAIRS - 1)]
    quarter = length >> 2
    length = length.astype(F32)
    inverse = 1.0 / jnp.full((16, LANES), length, F32)
    pairs = pair_v[...].reshape(1, SLOTS)
    for i in range(SLOTS // LANES):
        pair = pairs[:, i * LANES : (i + 1) * LANES]
        even = jnp.where((pair & 1) == 0, pair, TRUNC - 1 - pair).astype(F32)
        column = jnp.broadcast_to(even, (LANES, LANES)).T
        for start in range(i * LANES, 2 * SLOTS + LANES, SLOTS):
            waves[start : start + LANES, :] = column

    lane = lane_iota(16).astype(F32)
    left[...] = jnp.zeros_like(left)
    for _, count, padded, offset in ARRIVALS:
        used = count * SLOTS_DEV
        blank = jnp.zeros((2, padded - used, QUARTER_PAD), BF16)
        basis[:, offset + used : offset + padded, :] = blank
        basis[:, offset + padded + used : offset + 2 * padded, :] = blank

    for begin, count, padded, offset in ARRIVALS:

        def basis_rows(i, carry, begin=begin, padded=padded, offset=offset):
            at = pl.multiple_of(offset + i * 16, 16)
            low = pl.multiple_of(offset + padded + i * 16, 16)
            even = waves[pl.ds(SLOTS_DEV * (w + begin) + i * 16, 16), :]
            for parity in range(2):
                number = even if parity == 0 else (TRUNC - 1.0) - even
                factor = jnp.where(
                    2.0 * number < length, jnp.where(number == 0.0, 1.0, 2.0), 0.0
                )
                cosine, sine = unit_circle(number * lane, length, inverse)
                turn_cos, turn_sin = unit_circle(number * float(LANES), length, inverse)
                real = factor * cosine
                imag = -factor * sine
                for k in range(QUARTER_PAD // LANES):
                    columns = slice(k * LANES, (k + 1) * LANES)
                    basis[parity, pl.ds(at, 16), columns] = real.astype(BF16)
                    basis[parity, pl.ds(low, 16), columns] = imag.astype(BF16)
                    real, imag = (
                        real * turn_cos + imag * turn_sin,
                        imag * turn_cos - real * turn_sin,
                    )
            return carry

        lax.fori_loop(0, count * SLOTS_DEV // 16, basis_rows, 0)

    row = lax.broadcasted_iota(jnp.int32, (LANES, LANES), 0)
    wanted = jnp.where(row < 64, 2 * row, 2 * row - 127)
    pick = jnp.where(lane_iota(LANES) == wanted, 1.0, 0.0).astype(BF16)
    own.wait()
    for part, (begin, count, padded, offset) in enumerate(ARRIVALS):
        used = count * SLOTS_DEV
        held = pl.ds(0, count * LEV - (1 if part == 0 else 0))
        pltpu.make_async_copy(send.at[held], recv.at[held], recv_sem.at[part]).wait()
        column = waves[pl.ds(SLOTS_DEV * (w + begin), padded), :]
        evens = column.T[:1, :used].astype(jnp.int32)
        for parity in range(2):
            number = evens if parity == 0 else TRUNC - 1 - evens
            second = ((number >> 1) & 1).astype(F32)
            sign = 1.0 - 2.0 * second if parity == 0 else 2.0 * second - 1.0
            for lev in range(LEV):
                first = lev * WAVE + begin
                block = recv[first : first + count, parity * 5 : parity * 5 + 5]
                block = block.reshape(used, LANES)
                parts = lax.dot_general(pick, block, NT, preferred_element_type=F32)
                real, imag = parts[:64], parts[64:]
                top = slice(lev * 64, lev * 64 + 64)
                low = slice(256 + lev * 64, 256 + lev * 64 + 64)
                at = slice(offset, offset + used)
                after = slice(offset + padded, offset + padded + used)
                left[parity, top, at] = real.astype(BF16)
                left[parity, top, after] = imag.astype(BF16)
                if parity == 0:
                    left[parity, low, at] = (real * sign).astype(BF16)
                    left[parity, low, after] = (imag * sign).astype(BF16)
                else:
                    left[parity, low, at] = (imag * sign).astype(BF16)
                    left[parity, low, after] = (real * -sign).astype(BF16)
        terms = slice(offset, offset + 2 * padded)
        for number, (origin, width) in enumerate(COLUMN_BLOCKS):
            columns = slice(origin, origin + width)
            sums = [
                jnp.dot(
                    left[parity, :, terms],
                    basis[parity, terms, columns],
                    preferred_element_type=F32,
                )
                for parity in range(2)
            ]
            if part > 0:
                sums = [total[parity, :, columns] + sums[parity] for parity in range(2)]
            if part < len(ARRIVALS) - 1:
                for parity in range(2):
                    total[parity, :, columns] = sums[parity]
                continue
            even, odd = sums
            point = origin + lax.broadcasted_iota(jnp.int32, (256, width), 1)
            inside = point < quarter
            for c in range(4):
                half = slice((c & 1) * 256, (c & 1) * 256 + 256)
                value = even[half] + odd[half] if c < 2 else even[half] - odd[half]
                quarters[c, :, columns] = jnp.where(inside, value, 0.0).astype(BF16)
            pltpu.make_async_copy(
                quarters.at[:, :, pl.ds(origin, width)],
                quarters_out.at[:, :, pl.ds(origin, width)],
                out_sem.at[number],
            ).start()
    others = pl.ds(0, ROWS - 1)
    pltpu.make_async_copy(send.at[others], recv.at[others], send_sem).wait()
    for number, (origin, width) in enumerate(COLUMN_BLOCKS):
        pltpu.make_async_copy(
            quarters.at[:, :, pl.ds(origin, width)],
            quarters_out.at[:, :, pl.ds(origin, width)],
            out_sem.at[number],
        ).wait()


def place_kernel(row_s, length_s, quarters, grid_out):
    me = lax.axis_index("wave") * LEV + lax.axis_index("lev")
    quarter = length_s[row_s[me] & (PAIRS - 1)] >> 2
    grid_out[...] = jnp.zeros_like(grid_out)
    lane = lane_iota(ROW_CHUNK)
    tiles = QUARTER_PAD // LANES
    for c in range(4):
        offset = c * quarter
        shift = offset & (LANES - 1)
        start = pl.multiple_of(offset - shift, LANES)
        before = lane < shift
        previous = jnp.zeros((ROW_CHUNK, LANES), F32)
        for i in range(tiles + 1):
            if i < tiles:
                tile = quarters[c, :, i * LANES : (i + 1) * LANES].astype(F32)
                turned = pltpu.roll(tile, shift, 1)
            else:
                turned = jnp.zeros((ROW_CHUNK, LANES), F32)
            piece = jnp.where(before, previous, turned).astype(BF16)
            previous = turned
            where = pl.ds(pl.multiple_of(start + i * LANES, LANES), LANES)
            if i == 0:
                grid_out[0, :, where] += piece
            else:
                grid_out[0, :, where] = piece


def shards(spectral_even, spectral_odd, table_even, table_odd, slot_pair, slot_row, row_length):
    in_smem = pl.BlockSpec(memory_space=SMEM)
    in_vmem = pl.BlockSpec(memory_space=VMEM)
    anywhere = pl.BlockSpec(memory_space=pl.ANY)
    coefficients = (spectral_even, spectral_odd, table_even, table_odd)

    message = (MESSAGE // 2, 2, LANES)
    quarters = pl.pallas_call(
        exchange_kernel,
        out_shape=jax.ShapeDtypeStruct((4, 256, QUARTER_PAD), BF16),
        in_specs=[in_smem] * 3 + [in_vmem] * 2 + [anywhere] * 4,
        out_specs=anywhere,
        scratch_shapes=[VMEM(a.shape, BF16) for a in coefficients]
        + [
            VMEM((ROWS, ROWS), BF16),
            VMEM((ROWS * MESSAGE, LANES), F32),
            VMEM((ROWS,) + message, BF16),
            VMEM((ROWS,) + message, BF16),
            VMEM((2 * SLOTS + LANES, LANES), F32),
            VMEM((2, TERMS, QUARTER_PAD), BF16),
            VMEM((2, 512, TERMS), BF16),
            VMEM((2, 512, QUARTER_PAD), F32),
            VMEM((4, 256, QUARTER_PAD), BF16),
            pltpu.SemaphoreType.DMA,
            pltpu.SemaphoreType.DMA((len(ARRIVALS),)),
            pltpu.SemaphoreType.DMA,
            pltpu.SemaphoreType.DMA((4, len(LOADS))),
            pltpu.SemaphoreType.DMA((len(COLUMN_BLOCKS),)),
            pltpu.SemaphoreType.REGULAR,
        ],
        name="legendre_exchange_fourier",
        compiler_params=pltpu.CompilerParams(
            collective_id=0, has_side_effects=True, vmem_limit_bytes=60 << 20
        ),
        cost_estimate=pl.CostEstimate(
            flops=4 * 512 * TERMS * QUARTER_PAD, bytes_accessed=10 << 20, transcendentals=0
        ),
    )(
        slot_pair,
        slot_row,
        row_length,
        slot_pair,
        slot_row,
        *coefficients,
    )
    return pl.pallas_call(
        place_kernel,
        grid=(256 // ROW_CHUNK,),
        out_shape=jax.ShapeDtypeStruct((1, 256, LPAD), BF16),
        in_specs=[
            in_smem,
            in_smem,
            pl.BlockSpec((4, ROW_CHUNK, QUARTER_PAD), lambda i: (0, i, 0)),
        ],
        out_specs=pl.BlockSpec((1, ROW_CHUNK, LPAD), lambda i: (0, i, 0)),
        name="place",
        compiler_params=pltpu.CompilerParams(vmem_limit_bytes=60 << 20),
        cost_estimate=pl.CostEstimate(flops=1 << 22, bytes_accessed=6 << 20, transcendentals=0),
    )(slot_row, row_length, quarters)


def solution(mesh):
    in_specs = (
        P("wave", None, "lev"),
        P("wave", None, "lev"),
        P("wave", None, None),
        P("wave", None, None),
        P(),
        P(),
        P(),
    )
    out_specs = P(("wave", "lev"), None, None)
    return jax.shard_map(shards, mesh=mesh, in_specs=in_specs, out_specs=out_specs, check_vma=False)
```

```python
import math

import jax
import jax.numpy as jnp
from jax import lax
from jax.experimental import pallas as pl
from jax.experimental.pallas import tpu as pltpu
from jax.sharding import PartitionSpec as P

TRUNC = 1280
SLOTS = 640
LPAD = 5632
ROWS = 256
PAIRS = 128
WAVE = 64
LEV = 4
SLOTS_DEV = 10
MESSAGE = 2 * SLOTS_DEV
LOADS = ((0, 2), (2, 4), (6, 4))
QUARTER_PAD = 1408
LANES = 128
COLUMN_BLOCKS = ((0, 512), (512, 512), (1024, 256), (1280, 128))
ROW_CHUNK = 128
ARRIVALS = ((0, 36, 384, 0), (36, 16, 256, 768), (52, 12, 128, 1280))
TERMS = 1536
GROUP = 16
BARRIER_LOAD = 1

MESH = pl.DeviceIdType.MESH
VMEM = pltpu.VMEM
SMEM = pltpu.SMEM
F32 = jnp.float32
BF16 = jnp.bfloat16
TN = (((0,), (0,)), ((), ()))
NT = (((1,), (1,)), ((), ()))


def lane_iota(rows):
    return lax.broadcasted_iota(jnp.int32, (rows, LANES), 1)


def unit_circle(product, length, inverse):
    rest = product - jnp.floor(product * inverse) * length
    quarters = rest * (4.0 * inverse)
    nearest = jnp.floor(quarters + 0.5)
    angle = (quarters - nearest) * (0.5 * math.pi)
    z = angle * angle
    sine = angle * (1.0 + z * (-1.0 / 6 + z * (1.0 / 120 + z * (-1.0 / 5040 + z * (1.0 / 362880)))))
    cosine = 1.0 + z * (-0.5 + z * (1.0 / 24 + z * (-1.0 / 720 + z * (1.0 / 40320))))
    quadrant = nearest.astype(jnp.int32)
    odd = (quadrant & 1) == 1
    cos_out = jnp.where(odd, sine, cosine)
    sin_out = jnp.where(odd, cosine, sine)
    cos_out = jnp.where(((quadrant + 1) & 2) == 2, -cos_out, cos_out)
    sin_out = jnp.where((quadrant & 2) == 2, -sin_out, sin_out)
    return cos_out, sin_out


def masked_halves(coeffs, count, flip):
    rows = coeffs.shape[0]
    position = lax.broadcasted_iota(jnp.int32, (rows, LANES), 0)
    first = jnp.where(position < count, 1.0, 0.0)
    chosen = (flip + (1.0 - 2.0 * flip) * first).astype(BF16)
    even = coeffs * chosen
    return jnp.concatenate([even, coeffs - even], axis=1)


def exchange_kernel(
    pair_s,
    row_s,
    length_s,
    pair_v,
    row_v,
    spec_even_in,
    spec_odd_in,
    tab_even_in,
    tab_odd_in,
    quarters_out,
    spec_even,
    spec_odd,
    tab_even,
    tab_odd,
    permute,
    spread,
    send,
    recv,
    waves,
    basis,
    left,
    total,
    quarters,
    send_sem,
    recv_sem,
    self_sem,
    load_sem,
    out_sem,
    line_sem,
):
    w = lax.axis_index("wave")
    l = lax.axis_index("lev")
    me = w * LEV + l
    barrier = pltpu.get_barrier_semaphore()

    def in_plane(i):
        return (w - lax.rem(w, GROUP) + lax.rem(w + i, GROUP), l)

    def across(i):
        return (lax.rem(w + i // LEV * GROUP, WAVE), lax.rem(l + i, LEV))

    loads = []
    for number, (begin, count) in enumerate(LOADS):
        slots = pl.ds(begin, count)
        loads.append(
            [
                pltpu.make_async_copy(source.at[slots], held.at[slots], load_sem.at[i, number])
                for i, (source, held) in enumerate(
                    (
                        (spec_even_in, spec_even),
                        (tab_even_in, tab_even),
                        (spec_odd_in, spec_odd),
                        (tab_odd_in, tab_odd),
                    )
                )
            ]
        )
    for copy in loads[0]:
        copy.start()
    for i in range(1, GROUP):
        pl.semaphore_signal(barrier, inc=1, device_id=in_plane(i), device_id_type=MESH)
        pl.semaphore_signal(barrier, inc=1, device_id=across(i), device_id_type=MESH)
    for copies in loads[1:]:
        for copy in copies:
            copy.start()
    source = lax.broadcasted_iota(jnp.int32, (ROWS, ROWS), 0)
    hot = jnp.where(source == row_v[...].reshape(1, ROWS), 1.0, 0.0)
    permute[...] = hot.T.astype(BF16)

    def one_slot(slot):
        first = pair_s[w * SLOTS_DEV + slot]
        flip = (first & 1).astype(F32)
        even_terms = masked_halves(spec_even[slot], (TRUNC + 1 - first) >> 1, flip)
        odd_terms = masked_halves(spec_odd[slot], (TRUNC - first) >> 1, flip)
        sym = lax.dot_general(tab_even[slot], even_terms, TN, preferred_element_type=F32)
        anti = lax.dot_general(tab_odd[slot], odd_terms, TN, preferred_element_type=F32)
        rows = jnp.concatenate([sym + anti, sym - anti], axis=0).astype(BF16)
        ordered = jnp.dot(permute[...], rows, preferred_element_type=F32)
        spread[pl.ds(slot, ROWS, stride=MESSAGE), :] = ordered[:, :LANES]
        spread[pl.ds(slot + SLOTS_DEV, ROWS, stride=MESSAGE), :] = ordered[:, LANES:]

    for number, (begin, count) in enumerate(LOADS):
        for copy in loads[number]:
            copy.wait()

        def two_slots(i, carry, begin=begin):
            one_slot(begin + 2 * i)
            one_slot(begin + 2 * i + 1)
            return carry

        lax.fori_loop(0, count // 2, two_slots, 0)
        if number == BARRIER_LOAD:
            pl.semaphore_wait(barrier, 2 * (GROUP - 1))
            for i in range(1, GROUP):
                pl.semaphore_signal(line_sem, inc=1, device_id=across(i), device_id_type=MESH)

    pl.semaphore_wait(line_sem, GROUP - 1)

    def pack(back):
        target = lax.rem(w - back + WAVE, WAVE)
        start = pl.multiple_of(target * (LEV * MESSAGE), LEV * MESSAGE)
        block = spread[pl.ds(start, LEV * MESSAGE), :].astype(BF16)
        send[pl.ds(target * LEV, LEV)] = block.reshape(LEV, MESSAGE // 2, 2, LANES)
        return target

    def send_one(target, back, turn, part):
        lev = lax.rem(l - turn + LEV, LEV)
        pltpu.make_async_remote_copy(
            src_ref=send.at[target * LEV + lev],
            dst_ref=recv.at[l * WAVE + back],
            send_sem=send_sem,
            recv_sem=recv_sem.at[part],
            device_id=(target, lev),
            device_id_type=MESH,
        ).start()

    target = pack(0)
    for turn in range(1, LEV):
        send_one(target, 0, turn, 0)
    own = pltpu.make_async_copy(send.at[me], recv.at[l * WAVE], self_sem)
    own.start()
    for part, (begin, count, _, _) in enumerate(ARRIVALS):

        def send_four(back, carry, part=part):
            target = pack(back)
            for turn in range(LEV):
                send_one(target, back, turn, part)
            return carry

        lax.fori_loop(max(begin, 1), begin + count, send_four, 0)

    length = length_s[row_s[me] & (PAIRS - 1)]
    quarter = length >> 2
    length = length.astype(F32)
    inverse = 1.0 / jnp.full((16, LANES), length, F32)
    pairs = pair_v[...].reshape(1, SLOTS)
    for i in range(SLOTS // LANES):
        pair = pairs[:, i * LANES : (i + 1) * LANES]
        even = jnp.where((pair & 1) == 0, pair, TRUNC - 1 - pair).astype(F32)
        column = jnp.broadcast_to(even, (LANES, LANES)).T
        for start in range(i * LANES, 2 * SLOTS + LANES, SLOTS):
            waves[start : start + LANES, :] = column

    lane = lane_iota(16).astype(F32)
    row_number = lax.broadcasted_iota(jnp.int32, (16, LANES), 0)
    left[...] = jnp.zeros_like(left)
    for _, count, padded, offset in ARRIVALS:
        made = -(-count * SLOTS_DEV // 16) * 16
        if made < padded:
            blank = jnp.zeros((2, padded - made, QUARTER_PAD), BF16)
            basis[:, offset + made : offset + padded, :] = blank
            basis[:, offset + padded + made : offset + 2 * padded, :] = blank

    for begin, count, padded, offset in ARRIVALS:

        def basis_rows(i, carry, begin=begin, count=count, padded=padded, offset=offset):
            real_row = i * 16 + row_number < count * SLOTS_DEV
            at = pl.multiple_of(offset + i * 16, 16)
            low = pl.multiple_of(offset + padded + i * 16, 16)
            even = waves[pl.ds(SLOTS_DEV * (w + begin) + i * 16, 16), :]
            for parity in range(2):
                number = even if parity == 0 else (TRUNC - 1.0) - even
                active = (2.0 * number < length) & real_row
                factor = jnp.where(active, jnp.where(number == 0.0, 1.0, 2.0), 0.0)
                cosine, sine = unit_circle(number * lane, length, inverse)
                turn_cos, turn_sin = unit_circle(number * float(LANES), length, inverse)
                real = factor * cosine
                imag = -factor * sine
                for k in range(QUARTER_PAD // LANES):
                    columns = slice(k * LANES, (k + 1) * LANES)
                    basis[parity, pl.ds(at, 16), columns] = real.astype(BF16)
                    basis[parity, pl.ds(low, 16), columns] = imag.astype(BF16)
                    real, imag = (
                        real * turn_cos + imag * turn_sin,
                        imag * turn_cos - real * turn_sin,
                    )
            return carry

        lax.fori_loop(0, -(-count * SLOTS_DEV // 16), basis_rows, 0)

    row = lax.broadcasted_iota(jnp.int32, (LANES, LANES), 0)
    wanted = jnp.where(row < 64, 2 * row, 2 * row - 127)
    pick = jnp.where(lane_iota(LANES) == wanted, 1.0, 0.0).astype(BF16)
    own.wait()
    for part, (begin, count, padded, offset) in enumerate(ARRIVALS):
        used = count * SLOTS_DEV
        held = pl.ds(0, count * LEV - (1 if part == 0 else 0))
        pltpu.make_async_copy(send.at[held], recv.at[held], recv_sem.at[part]).wait()
        column = waves[pl.ds(SLOTS_DEV * (w + begin), padded), :]
        evens = column.T[:1, :used].astype(jnp.int32)
        for parity in range(2):
            number = evens if parity == 0 else TRUNC - 1 - evens
            second = ((number >> 1) & 1).astype(F32)
            sign = 1.0 - 2.0 * second if parity == 0 else 2.0 * second - 1.0
            for lev in range(LEV):
                first = lev * WAVE + begin
                block = recv[first : first + count, parity * 5 : parity * 5 + 5]
                block = block.reshape(used, LANES)
                parts = lax.dot_general(pick, block, NT, preferred_element_type=F32)
                real, imag = parts[:64], parts[64:]
                top = slice(lev * 64, lev * 64 + 64)
                low = slice(256 + lev * 64, 256 + lev * 64 + 64)
                at = slice(offset, offset + used)
                after = slice(offset + padded, offset + padded + used)
                left[parity, top, at] = real.astype(BF16)
                left[parity, top, after] = imag.astype(BF16)
                if parity == 0:
                    left[parity, low, at] = (real * sign).astype(BF16)
                    left[parity, low, after] = (imag * sign).astype(BF16)
                else:
                    left[parity, low, at] = (imag * sign).astype(BF16)
                    left[parity, low, after] = (real * -sign).astype(BF16)
        terms = slice(offset, offset + 2 * padded)
        for number, (origin, width) in enumerate(COLUMN_BLOCKS):
            columns = slice(origin, origin + width)
            sums = [
                jnp.dot(
                    left[parity, :, terms],
                    basis[parity, terms, columns],
                    preferred_element_type=F32,
                )
                for parity in range(2)
            ]
            if part > 0:
                sums = [total[parity, :, columns] + sums[parity] for parity in range(2)]
            if part < len(ARRIVALS) - 1:
                for parity in range(2):
                    total[parity, :, columns] = sums[parity]
                continue
            even, odd = sums
            point = origin + lax.broadcasted_iota(jnp.int32, (256, width), 1)
            inside = point < quarter
            for c in range(4):
                half = slice((c & 1) * 256, (c & 1) * 256 + 256)
                value = even[half] + odd[half] if c < 2 else even[half] - odd[half]
                quarters[c, :, columns] = jnp.where(inside, value, 0.0).astype(BF16)
            pltpu.make_async_copy(
                quarters.at[:, :, pl.ds(origin, width)],
                quarters_out.at[:, :, pl.ds(origin, width)],
                out_sem.at[number],
            ).start()
    others = pl.ds(0, ROWS - 1)
    pltpu.make_async_copy(send.at[others], recv.at[others], send_sem).wait()
    for number, (origin, width) in enumerate(COLUMN_BLOCKS):
        pltpu.make_async_copy(
            quarters.at[:, :, pl.ds(origin, width)],
            quarters_out.at[:, :, pl.ds(origin, width)],
            out_sem.at[number],
        ).wait()


def place_kernel(row_s, length_s, quarters, grid_out):
    me = lax.axis_index("wave") * LEV + lax.axis_index("lev")
    quarter = length_s[row_s[me] & (PAIRS - 1)] >> 2
    grid_out[...] = jnp.zeros_like(grid_out)
    lane = lane_iota(ROW_CHUNK)
    tiles = QUARTER_PAD // LANES
    for c in range(4):
        offset = c * quarter
        shift = offset & (LANES - 1)
        start = pl.multiple_of(offset - shift, LANES)
        before = lane < shift
        previous = jnp.zeros((ROW_CHUNK, LANES), BF16)
        for i in range(tiles + 1):
            if i < tiles:
                tile = quarters[c, :, i * LANES : (i + 1) * LANES]
                turned = pltpu.roll(tile, shift, 1)
            else:
                turned = jnp.zeros((ROW_CHUNK, LANES), BF16)
            piece = jnp.where(before, previous, turned)
            previous = turned
            where = pl.ds(pl.multiple_of(start + i * LANES, LANES), LANES)
            if i == 0:
                grid_out[0, :, where] += piece
            else:
                grid_out[0, :, where] = piece


def shards(spectral_even, spectral_odd, table_even, table_odd, slot_pair, slot_row, row_length):
    in_smem = pl.BlockSpec(memory_space=SMEM)
    in_vmem = pl.BlockSpec(memory_space=VMEM)
    anywhere = pl.BlockSpec(memory_space=pl.ANY)
    coefficients = (spectral_even, spectral_odd, table_even, table_odd)

    message = (MESSAGE // 2, 2, LANES)
    quarters = pl.pallas_call(
        exchange_kernel,
        out_shape=jax.ShapeDtypeStruct((4, 256, QUARTER_PAD), BF16),
        in_specs=[in_smem] * 3 + [in_vmem] * 2 + [anywhere] * 4,
        out_specs=anywhere,
        scratch_shapes=[VMEM(a.shape, BF16) for a in coefficients]
        + [
            VMEM((ROWS, ROWS), BF16),
            VMEM((ROWS * MESSAGE, LANES), F32),
            VMEM((ROWS,) + message, BF16),
            VMEM((ROWS,) + message, BF16),
            VMEM((2 * SLOTS + LANES, LANES), F32),
            VMEM((2, TERMS, QUARTER_PAD), BF16),
            VMEM((2, 512, TERMS), BF16),
            VMEM((2, 512, QUARTER_PAD), F32),
            VMEM((4, 256, QUARTER_PAD), BF16),
            pltpu.SemaphoreType.DMA,
            pltpu.SemaphoreType.DMA((len(ARRIVALS),)),
            pltpu.SemaphoreType.DMA,
            pltpu.SemaphoreType.DMA((4, len(LOADS))),
            pltpu.SemaphoreType.DMA((len(COLUMN_BLOCKS),)),
            pltpu.SemaphoreType.REGULAR,
        ],
        name="legendre_exchange_fourier",
        compiler_params=pltpu.CompilerParams(
            collective_id=0, has_side_effects=True, vmem_limit_bytes=60 << 20
        ),
        cost_estimate=pl.CostEstimate(
            flops=4 * 512 * TERMS * QUARTER_PAD, bytes_accessed=10 << 20, transcendentals=0
        ),
    )(
        slot_pair,
        slot_row,
        row_length,
        slot_pair,
        slot_row,
        *coefficients,
    )
    return pl.pallas_call(
        place_kernel,
        grid=(256 // ROW_CHUNK,),
        out_shape=jax.ShapeDtypeStruct((1, 256, LPAD), BF16),
        in_specs=[
            in_smem,
            in_smem,
            pl.BlockSpec((4, ROW_CHUNK, QUARTER_PAD), lambda i: (0, i, 0)),
        ],
        out_specs=pl.BlockSpec((1, ROW_CHUNK, LPAD), lambda i: (0, i, 0)),
        name="place",
        compiler_params=pltpu.CompilerParams(vmem_limit_bytes=60 << 20),
        cost_estimate=pl.CostEstimate(flops=1 << 22, bytes_accessed=6 << 20, transcendentals=0),
    )(slot_row, row_length, quarters)


def solution(mesh):
    in_specs = (
        P("wave", None, "lev"),
        P("wave", None, "lev"),
        P("wave", None, None),
        P("wave", None, None),
        P(),
        P(),
        P(),
    )
    out_specs = P(("wave", "lev"), None, None)
    return jax.shard_map(shards, mesh=mesh, in_specs=in_specs, out_specs=out_specs, check_vma=False)
```

```python
import math

import jax
import jax.numpy as jnp
from jax import lax
from jax.experimental import pallas as pl
from jax.experimental.pallas import tpu as pltpu
from jax.sharding import PartitionSpec as P

TRUNC = 1280
SLOTS = 640
LPAD = 5632
ROWS = 256
PAIRS = 128
WAVE = 64
LEV = 4
SLOTS_DEV = 10
MESSAGE = 2 * SLOTS_DEV
STEP_SLOTS = 2
STEPS = SLOTS_DEV // STEP_SLOTS
QUARTER_PAD = 1408
LANES = 128
COLUMN_BLOCKS = ((0, 512), (512, 512), (1024, 256), (1280, 128))
ROW_CHUNK = 128
ARRIVALS = ((0, 36, 384, 0), (36, 16, 256, 768), (52, 12, 128, 1280))
TERMS = 1536
GROUP = 16
BARRIER_STEP = 3

MESH = pl.DeviceIdType.MESH
VMEM = pltpu.VMEM
SMEM = pltpu.SMEM
F32 = jnp.float32
BF16 = jnp.bfloat16
TN = (((0,), (0,)), ((), ()))
NT = (((1,), (1,)), ((), ()))


def lane_iota(rows):
    return lax.broadcasted_iota(jnp.int32, (rows, LANES), 1)


def unit_circle(product, length, inverse):
    rest = product - jnp.floor(product * inverse) * length
    quarters = rest * (4.0 * inverse)
    nearest = jnp.floor(quarters + 0.5)
    angle = (quarters - nearest) * (0.5 * math.pi)
    z = angle * angle
    sine = angle * (1.0 + z * (-1.0 / 6 + z * (1.0 / 120 + z * (-1.0 / 5040 + z * (1.0 / 362880)))))
    cosine = 1.0 + z * (-0.5 + z * (1.0 / 24 + z * (-1.0 / 720 + z * (1.0 / 40320))))
    quadrant = nearest.astype(jnp.int32)
    odd = (quadrant & 1) == 1
    cos_out = jnp.where(odd, sine, cosine)
    sin_out = jnp.where(odd, cosine, sine)
    cos_out = jnp.where(((quadrant + 1) & 2) == 2, -cos_out, cos_out)
    sin_out = jnp.where((quadrant & 2) == 2, -sin_out, sin_out)
    return cos_out, sin_out


def masked_halves(coeffs, count, flip):
    rows = coeffs.shape[0]
    position = lax.broadcasted_iota(jnp.int32, (rows, LANES), 0)
    first = jnp.where(position < count, 1.0, 0.0)
    chosen = (flip + (1.0 - 2.0 * flip) * first).astype(BF16)
    even = coeffs * chosen
    return jnp.concatenate([even, coeffs - even], axis=1)


def exchange_kernel(
    pair_s,
    row_s,
    length_s,
    pair_v,
    row_v,
    spec_even,
    spec_odd,
    tab_even,
    tab_odd,
    quarters_out,
    permute,
    spread,
    send,
    recv,
    waves,
    basis,
    left,
    total,
    quarters,
    send_sem,
    recv_sem,
    self_sem,
    out_sem,
    line_sem,
):
    step = pl.program_id(0)
    w = lax.axis_index("wave")
    l = lax.axis_index("lev")
    me = w * LEV + l
    barrier = pltpu.get_barrier_semaphore()

    def in_plane(i):
        return (w - lax.rem(w, GROUP) + lax.rem(w + i, GROUP), l)

    def across(i):
        return (lax.rem(w + i // LEV * GROUP, WAVE), lax.rem(l + i, LEV))

    @pl.when(step == 0)
    def _():
        for i in range(1, GROUP):
            pl.semaphore_signal(barrier, inc=1, device_id=in_plane(i), device_id_type=MESH)
            pl.semaphore_signal(barrier, inc=1, device_id=across(i), device_id_type=MESH)
        source = lax.broadcasted_iota(jnp.int32, (ROWS, ROWS), 0)
        hot = jnp.where(source == row_v[...].reshape(1, ROWS), 1.0, 0.0)
        permute[...] = hot.T.astype(BF16)

    @pl.when(step == BARRIER_STEP)
    def _():
        pl.semaphore_wait(barrier, 2 * (GROUP - 1))
        for i in range(1, GROUP):
            pl.semaphore_signal(line_sem, inc=1, device_id=across(i), device_id_type=MESH)

    for j in range(STEP_SLOTS):
        slot = step * STEP_SLOTS + j
        first = pair_s[w * SLOTS_DEV + slot]
        flip = (first & 1).astype(F32)
        even_terms = masked_halves(spec_even[j], (TRUNC + 1 - first) >> 1, flip)
        odd_terms = masked_halves(spec_odd[j], (TRUNC - first) >> 1, flip)
        sym = lax.dot_general(tab_even[j], even_terms, TN, preferred_element_type=F32)
        anti = lax.dot_general(tab_odd[j], odd_terms, TN, preferred_element_type=F32)
        rows = jnp.concatenate([sym + anti, sym - anti], axis=0).astype(BF16)
        ordered = jnp.dot(permute[...], rows, preferred_element_type=F32)
        spread[pl.ds(slot, ROWS, stride=MESSAGE), :] = ordered[:, :LANES]
        spread[pl.ds(slot + SLOTS_DEV, ROWS, stride=MESSAGE), :] = ordered[:, LANES:]

    @pl.when(step == STEPS - 1)
    def _():
        pl.semaphore_wait(line_sem, GROUP - 1)

        def pack(back):
            target = lax.rem(w - back + WAVE, WAVE)
            start = pl.multiple_of(target * (LEV * MESSAGE), LEV * MESSAGE)
            block = spread[pl.ds(start, LEV * MESSAGE), :].astype(BF16)
            send[pl.ds(target * LEV, LEV)] = block.reshape(LEV, MESSAGE // 2, 2, LANES)
            return target

        def send_one(target, back, turn, part):
            lev = lax.rem(l - turn + LEV, LEV)
            pltpu.make_async_remote_copy(
                src_ref=send.at[target * LEV + lev],
                dst_ref=recv.at[l * WAVE + back],
                send_sem=send_sem,
                recv_sem=recv_sem.at[part],
                device_id=(target, lev),
                device_id_type=MESH,
            ).start()

        target = pack(0)
        for turn in range(1, LEV):
            send_one(target, 0, turn, 0)
        own = pltpu.make_async_copy(send.at[me], recv.at[l * WAVE], self_sem)
        own.start()
        for part, (begin, count, _, _) in enumerate(ARRIVALS):

            def send_four(back, carry, part=part):
                target = pack(back)
                for turn in range(LEV):
                    send_one(target, back, turn, part)
                return carry

            lax.fori_loop(max(begin, 1), begin + count, send_four, 0)

        length = length_s[row_s[me] & (PAIRS - 1)]
        quarter = length >> 2
        length = length.astype(F32)
        inverse = 1.0 / jnp.full((16, LANES), length, F32)
        pairs = pair_v[...].reshape(1, SLOTS)
        for i in range(SLOTS // LANES):
            pair = pairs[:, i * LANES : (i + 1) * LANES]
            even = jnp.where((pair & 1) == 0, pair, TRUNC - 1 - pair).astype(F32)
            column = jnp.broadcast_to(even, (LANES, LANES)).T
            for start in range(i * LANES, 2 * SLOTS + LANES, SLOTS):
                waves[start : start + LANES, :] = column

        lane = lane_iota(16).astype(F32)
        row_number = lax.broadcasted_iota(jnp.int32, (16, LANES), 0)
        left[...] = jnp.zeros_like(left)
        for _, count, padded, offset in ARRIVALS:
            made = -(-count * SLOTS_DEV // 16) * 16
            if made < padded:
                blank = jnp.zeros((2, padded - made, QUARTER_PAD), BF16)
                basis[:, offset + made : offset + padded, :] = blank
                basis[:, offset + padded + made : offset + 2 * padded, :] = blank

        for begin, count, padded, offset in ARRIVALS:

            def basis_rows(i, carry, begin=begin, count=count, padded=padded, offset=offset):
                real_row = i * 16 + row_number < count * SLOTS_DEV
                at = pl.multiple_of(offset + i * 16, 16)
                low = pl.multiple_of(offset + padded + i * 16, 16)
                even = waves[pl.ds(SLOTS_DEV * (w + begin) + i * 16, 16), :]
                for parity in range(2):
                    number = even if parity == 0 else (TRUNC - 1.0) - even
                    active = (2.0 * number < length) & real_row
                    factor = jnp.where(active, jnp.where(number == 0.0, 1.0, 2.0), 0.0)
                    cosine, sine = unit_circle(number * lane, length, inverse)
                    turn_cos, turn_sin = unit_circle(number * float(LANES), length, inverse)
                    real = factor * cosine
                    imag = -factor * sine
                    for k in range(QUARTER_PAD // LANES):
                        columns = slice(k * LANES, (k + 1) * LANES)
                        basis[parity, pl.ds(at, 16), columns] = real.astype(BF16)
                        basis[parity, pl.ds(low, 16), columns] = imag.astype(BF16)
                        real, imag = (
                            real * turn_cos + imag * turn_sin,
                            imag * turn_cos - real * turn_sin,
                        )
                return carry

            lax.fori_loop(0, -(-count * SLOTS_DEV // 16), basis_rows, 0)

        row = lax.broadcasted_iota(jnp.int32, (LANES, LANES), 0)
        wanted = jnp.where(row < 64, 2 * row, 2 * row - 127)
        pick = jnp.where(lane_iota(LANES) == wanted, 1.0, 0.0).astype(BF16)
        own.wait()
        for part, (begin, count, padded, offset) in enumerate(ARRIVALS):
            used = count * SLOTS_DEV
            held = pl.ds(0, count * LEV - (1 if part == 0 else 0))
            pltpu.make_async_copy(send.at[held], recv.at[held], recv_sem.at[part]).wait()
            column = waves[pl.ds(SLOTS_DEV * (w + begin), padded), :]
            evens = column.T[:1, :used].astype(jnp.int32)
            for parity in range(2):
                number = evens if parity == 0 else TRUNC - 1 - evens
                second = ((number >> 1) & 1).astype(F32)
                sign = 1.0 - 2.0 * second if parity == 0 else 2.0 * second - 1.0
                for lev in range(LEV):
                    first = lev * WAVE + begin
                    block = recv[first : first + count, parity * 5 : parity * 5 + 5]
                    block = block.reshape(used, LANES)
                    parts = lax.dot_general(pick, block, NT, preferred_element_type=F32)
                    real, imag = parts[:64], parts[64:]
                    top = slice(lev * 64, lev * 64 + 64)
                    low = slice(256 + lev * 64, 256 + lev * 64 + 64)
                    at = slice(offset, offset + used)
                    after = slice(offset + padded, offset + padded + used)
                    left[parity, top, at] = real.astype(BF16)
                    left[parity, top, after] = imag.astype(BF16)
                    if parity == 0:
                        left[parity, low, at] = (real * sign).astype(BF16)
                        left[parity, low, after] = (imag * sign).astype(BF16)
                    else:
                        left[parity, low, at] = (imag * sign).astype(BF16)
                        left[parity, low, after] = (real * -sign).astype(BF16)
            terms = slice(offset, offset + 2 * padded)
            for number, (origin, width) in enumerate(COLUMN_BLOCKS):
                columns = slice(origin, origin + width)
                sums = [
                    jnp.dot(
                        left[parity, :, terms],
                        basis[parity, terms, columns],
                        preferred_element_type=F32,
                    )
                    for parity in range(2)
                ]
                if part > 0:
                    sums = [total[parity, :, columns] + sums[parity] for parity in range(2)]
                if part < len(ARRIVALS) - 1:
                    for parity in range(2):
                        total[parity, :, columns] = sums[parity]
                    continue
                even, odd = sums
                point = origin + lax.broadcasted_iota(jnp.int32, (256, width), 1)
                inside = point < quarter
                for c in range(4):
                    half = slice((c & 1) * 256, (c & 1) * 256 + 256)
                    value = even[half] + odd[half] if c < 2 else even[half] - odd[half]
                    quarters[c, :, columns] = jnp.where(inside, value, 0.0).astype(BF16)
                pltpu.make_async_copy(
                    quarters.at[:, :, pl.ds(origin, width)],
                    quarters_out.at[:, :, pl.ds(origin, width)],
                    out_sem.at[number],
                ).start()
        others = pl.ds(0, ROWS - 1)
        pltpu.make_async_copy(send.at[others], recv.at[others], send_sem).wait()
        for number, (origin, width) in enumerate(COLUMN_BLOCKS):
            pltpu.make_async_copy(
                quarters.at[:, :, pl.ds(origin, width)],
                quarters_out.at[:, :, pl.ds(origin, width)],
                out_sem.at[number],
            ).wait()


def place_kernel(row_s, length_s, quarters, grid_out):
    me = lax.axis_index("wave") * LEV + lax.axis_index("lev")
    quarter = length_s[row_s[me] & (PAIRS - 1)] >> 2
    grid_out[...] = jnp.zeros_like(grid_out)
    lane = lane_iota(ROW_CHUNK)
    tiles = QUARTER_PAD // LANES
    for c in range(4):
        offset = c * quarter
        shift = offset & (LANES - 1)
        start = pl.multiple_of(offset - shift, LANES)
        before = lane < shift
        previous = jnp.zeros((ROW_CHUNK, LANES), BF16)
        for i in range(tiles + 1):
            if i < tiles:
                tile = quarters[c, :, i * LANES : (i + 1) * LANES]
                turned = pltpu.roll(tile, shift, 1)
            else:
                turned = jnp.zeros((ROW_CHUNK, LANES), BF16)
            piece = jnp.where(before, previous, turned)
            previous = turned
            where = pl.ds(pl.multiple_of(start + i * LANES, LANES), LANES)
            if i == 0:
                grid_out[0, :, where] += piece
            else:
                grid_out[0, :, where] = piece


def shards(spectral_even, spectral_odd, table_even, table_odd, slot_pair, slot_row, row_length):
    in_smem = pl.BlockSpec(memory_space=SMEM)
    in_vmem = pl.BlockSpec(memory_space=VMEM)
    anywhere = pl.BlockSpec(memory_space=pl.ANY)

    def by_slot(array):
        return pl.BlockSpec((STEP_SLOTS,) + array.shape[1:], lambda i: (i, 0, 0))

    message = (MESSAGE // 2, 2, LANES)
    quarters = pl.pallas_call(
        exchange_kernel,
        grid=(STEPS,),
        out_shape=jax.ShapeDtypeStruct((4, 256, QUARTER_PAD), BF16),
        in_specs=[in_smem] * 3
        + [in_vmem] * 2
        + [by_slot(a) for a in (spectral_even, spectral_odd, table_even, table_odd)],
        out_specs=anywhere,
        scratch_shapes=[
            VMEM((ROWS, ROWS), BF16),
            VMEM((ROWS * MESSAGE + MESSAGE, LANES), F32),
            VMEM((ROWS,) + message, BF16),
            VMEM((ROWS,) + message, BF16),
            VMEM((2 * SLOTS + LANES, LANES), F32),
            VMEM((2, TERMS, QUARTER_PAD), BF16),
            VMEM((2, 512, TERMS), BF16),
            VMEM((2, 512, QUARTER_PAD), F32),
            VMEM((4, 256, QUARTER_PAD), BF16),
            pltpu.SemaphoreType.DMA,
            pltpu.SemaphoreType.DMA((len(ARRIVALS),)),
            pltpu.SemaphoreType.DMA,
            pltpu.SemaphoreType.DMA((len(COLUMN_BLOCKS),)),
            pltpu.SemaphoreType.REGULAR,
        ],
        name="legendre_exchange_fourier",
        compiler_params=pltpu.CompilerParams(
            collective_id=0, has_side_effects=True, vmem_limit_bytes=60 << 20
        ),
        cost_estimate=pl.CostEstimate(
            flops=4 * 512 * TERMS * QUARTER_PAD, bytes_accessed=10 << 20, transcendentals=0
        ),
    )(
        slot_pair,
        slot_row,
        row_length,
        slot_pair,
        slot_row,
        spectral_even,
        spectral_odd,
        table_even,
        table_odd,
    )
    return pl.pallas_call(
        place_kernel,
        grid=(256 // ROW_CHUNK,),
        out_shape=jax.ShapeDtypeStruct((1, 256, LPAD), BF16),
        in_specs=[
            in_smem,
            in_smem,
            pl.BlockSpec((4, ROW_CHUNK, QUARTER_PAD), lambda i: (0, i, 0)),
        ],
        out_specs=pl.BlockSpec((1, ROW_CHUNK, LPAD), lambda i: (0, i, 0)),
        name="place",
        compiler_params=pltpu.CompilerParams(vmem_limit_bytes=60 << 20),
        cost_estimate=pl.CostEstimate(flops=1 << 22, bytes_accessed=6 << 20, transcendentals=0),
    )(slot_row, row_length, quarters)


def solution(mesh):
    in_specs = (
        P("wave", None, "lev"),
        P("wave", None, "lev"),
        P("wave", None, None),
        P("wave", None, None),
        P(),
        P(),
        P(),
    )
    out_specs = P(("wave", "lev"), None, None)
    return jax.shard_map(shards, mesh=mesh, in_specs=in_specs, out_specs=out_specs, check_vma=False)
```
